512 devices in a mesh: rep: 32 (over y_lo, z), fsdp: 16 (over x, y_hi, core).
Axes of the slice: x: 4, y: 4 (y_hi: 2, y_lo: 2; y = y_hi * 2 + y_lo), z: 16, core: 2. Of those that a mesh axis runs over, the one named last changes fastest.
Arguments:
- acts: bfloat16 [98304, 4096], P(('rep', 'fsdp')), may hold values from -24 to 24
- grad_out: bfloat16 [98304, 512], P(('rep', 'fsdp')), may hold values from -0.25 to 0.25
- inner_weight: bfloat16 [32, 4096, 512], P('rep', 'fsdp'), may hold values from -6 to 6
- adam_first: bfloat16 [32, 4096, 512], P('rep', 'fsdp'), may hold values from -6 to 6
- adam_second: bfloat16 [32, 4096, 512], P('rep', 'fsdp'), may hold values from 0.5 to 8
- global_weight: float32 [16, 32, 8, 512], P('fsdp', 'rep'), may hold values from -6 to 6
- outer_momentum: float32 [16, 32, 8, 512], P('fsdp', 'rep'), may hold values from -4 to 4
Outputs:
- input_grad: bfloat16 [98304, 4096], P(('rep', 'fsdp'))
- new_weight: bfloat16 [32, 4096, 512], P('rep', 'fsdp')
- new_first: bfloat16 [32, 4096, 512], P('rep', 'fsdp')
- new_second: bfloat16 [32, 4096, 512], P('rep', 'fsdp')
- new_global: float32 [16, 32, 8, 512], P('fsdp', 'rep')
- new_momentum: float32 [16, 32, 8, 512], P('fsdp', 'rep')
The draws below stay inside these ranges and needn't reach their ends.
All inputs are finite; a program needn't handle non-finite values.
Results may differ from the reference program's by a relative error of at most 0.015.
Values may be sent and summed in bfloat16 or wider, within the bound.
No kernel may reach another device: no remote copies, remote signals or barrier semaphores. Data moves between devices by JAX's collectives and lax.ppermute only.
A program may use at most 64 MiB of HBM per device.

```python
import math
import jax
import jax.numpy as jnp
from jax import lax

DW = 4096
KV = 512
TOK_DEV = 192
STEP = 10
TOKENS = 98304
SUB = 8
N_REP = 32
N_FSDP = 16


def raised(array, key, source, target, blocks, factor):
    def block_of(dim):
        return (jnp.arange(array.shape[dim]) // (array.shape[dim] // blocks)).reshape((-1,) + (1,) * (array.ndim - 1 - dim))

    one_side = jax.random.permutation(key, blocks)[block_of(target)]
    second = (block_of(target) + blocks // 2) % blocks
    return jnp.where((block_of(source) == one_side) | (block_of(source) == second), factor * array, array)


def block_levels(stream_key, shape, pieces, least, top_value):
    gain, own = 1.0, jax.random.fold_in(stream_key, 6)
    for position, parts in pieces:
        steps = jnp.exp(jax.random.uniform(jax.random.fold_in(own, position), (parts,), jnp.float32, least / len(pieces), top_value / len(pieces)))
        gain = gain * jnp.repeat(steps, shape[position] // parts).reshape([-1 if axis == position else 1 for axis in range(len(shape))])
    return gain


def scatter_about(stream_key, extent, width, most, pieces=(), kind=jnp.bfloat16):
    array = jax.random.normal(stream_key, extent, jnp.float32) * width
    if len(pieces) > 0:
        array = block_levels(stream_key, extent, pieces, -0.22, 0.18) * array
    return jnp.clip(array, min=-most, max=most).astype(kind)


def bell_draw_with(rng, extent, scale, most, cuts, heavy, dtype=jnp.bfloat16):
    result = scale * jax.random.normal(rng, extent, jnp.float32)
    if cuts:
        result = result * block_levels(rng, extent, cuts, -0.22, 0.18)
    return jnp.clip(raised(result, jax.random.fold_in(rng, 3), *heavy), -most, most).astype(dtype)


def setup_inputs(seed: int = 0) -> dict:
    streams_of = jax.random.split(jax.random.key(seed), 8)
    acts = bell_draw_with(streams_of[0], (TOKENS, DW), 1.0, 24.0, ((0, 512),), (0, 1, 512, 6.0))
    grad_out = scatter_about(streams_of[1], (TOKENS, KV), KV ** -0.5, 0.25, ((0, 512),))
    inner_weight = scatter_about(streams_of[2], (N_REP, DW, KV), 1.0, 6.0, ((0, 32), (1, 16)))
    adam_first = scatter_about(streams_of[3], (N_REP, DW, KV), 1.0, 6.0, ((0, 32), (1, 16)))
    adam_second = jnp.clip(jnp.exp(math.log(8.0) - 2.7725887 * jax.random.uniform(streams_of[4], (N_REP, DW, KV), jnp.float32) ** block_levels(streams_of[4], (N_REP, DW, KV), ((0, 32), (1, 16)), -0.2, 0.2)), 0.5, 8.0).astype(jnp.bfloat16)
    global_weight = scatter_about(streams_of[5], (N_FSDP, N_REP, SUB, KV), 1.0, 6.0, ((0, 16), (1, 32)), jnp.float32)
    outer_momentum = scatter_about(streams_of[6], (N_FSDP, N_REP, SUB, KV), 0.5, 4.0, ((0, 16), (1, 32)), jnp.float32)
    return dict(acts=acts, grad_out=grad_out, inner_weight=inner_weight, adam_first=adam_first, adam_second=adam_second, global_weight=global_weight, outer_momentum=outer_momentum)


momentum_coef = 0.9
outer_rate = 0.7
beta_first = 0.9
beta_second = 0.95
inner_rate = 0.25
decay_rate = 0.1
epsilon_adam = 1e-08
mix_factor = 0.5

def reference(acts, grad_out, inner_weight, adam_first, adam_second, global_weight, outer_momentum):
    tok_rep = TOK_DEV * N_FSDP
    act_groups = acts.reshape(N_REP, N_FSDP, TOK_DEV, DW)
    cot_groups = grad_out.reshape(N_REP, N_FSDP, TOK_DEV, KV)

    def replica_grad(pair):

        def add_group(carry, group):
            term = jnp.dot(group[0].T, group[1], preferred_element_type=jnp.float32)
            rounded = lax.optimization_barrier(term.astype(jnp.bfloat16))
            return (carry + rounded.astype(jnp.float32), None)
        total, unused = lax.scan(add_group, jnp.zeros((DW, KV), jnp.float32), pair)
        return total
    grads = lax.map(replica_grad, (act_groups, cot_groups))

    def replica_input(pair):
        return jnp.dot(pair[0], pair[1].T, preferred_element_type=jnp.float32).astype(jnp.bfloat16)
    input_grad = lax.map(replica_input, (grad_out.reshape(N_REP, tok_rep, KV), inner_weight)).reshape(TOKENS, DW)
    weight_wide = inner_weight.astype(jnp.float32)
    weight_mean = lax.optimization_barrier(jnp.sum(weight_wide, axis=0)) / N_REP
    global_mat = global_weight.reshape(DW, KV)
    outer_delta = global_mat - weight_mean
    momentum_new = momentum_coef * outer_momentum.reshape(DW, KV) + outer_delta
    global_new = global_mat - outer_rate * (outer_delta + momentum_coef * momentum_new)
    first = beta_first * adam_first.astype(jnp.float32) + (1.0 - beta_first) * grads
    second = beta_second * adam_second.astype(jnp.float32) + (1.0 - beta_second) * grads * grads
    first_hat = first / (1.0 - beta_first ** STEP)
    second_hat = second / (1.0 - beta_second ** STEP)
    adamw = weight_wide - inner_rate * (first_hat / (jnp.sqrt(second_hat) + epsilon_adam) + decay_rate * weight_wide)
    new_weight = (mix_factor * adamw + (1.0 - mix_factor) * global_new[None]).astype(jnp.bfloat16)
    shape_outer = global_weight.shape
    return (input_grad, new_weight, first.astype(jnp.bfloat16), second.astype(jnp.bfloat16), global_new.reshape(shape_outer), momentum_new.reshape(shape_outer))
```

```python
import functools

import jax
import jax.numpy as jnp
from jax import lax
from jax.experimental import pallas as pl
from jax.experimental.pallas import tpu as pltpu
from jax.sharding import Mesh, PartitionSpec as P

STEP = 10

momentum_coef = 0.9
outer_rate = 0.7
beta_first = 0.9
beta_second = 0.95
inner_rate = 0.25
decay_rate = 0.1
epsilon_adam = 1e-08
mix_factor = 0.5

AXES = ("ylo", "zhi", "zlo", "x", "yhi", "core")
SIZES = (2, 4, 4, 4, 2, 2)
REP = ("ylo", "zhi", "zlo")
FSDP = ("x", "yhi", "core")
BF = jnp.bfloat16
F32 = jnp.float32


def permute(array, axis, size, shift):
    return lax.ppermute(array, axis, [(i, (i + shift) % size) for i in range(size)])


SCALE = outer_rate * (1.0 + momentum_coef) / 32


def share_of(globe, momentum):
    return (1.0 - outer_rate * (1.0 + momentum_coef)) * globe - (
        outer_rate * momentum_coef * momentum_coef
    ) * momentum


def call(kernel, operands, out_shape, name, loose=0, scratch=(), space=pl.ANY, weight=0, limit=40):
    fixed = len(operands) - loose
    return pl.pallas_call(
        kernel,
        in_specs=[pl.BlockSpec(memory_space=pltpu.VMEM)] * fixed
        + [pl.BlockSpec(memory_space=space)] * loose,
        out_shape=out_shape,
        scratch_shapes=scratch,
        compiler_params=pltpu.CompilerParams(vmem_limit_bytes=limit * 2**20),
        cost_estimate=pl.CostEstimate(flops=weight, bytes_accessed=2**18, transcendentals=0),
        name=name,
    )(*operands)


def shaped(*shape):
    return jax.ShapeDtypeStruct(shape, BF)


def column(block):
    return pl.ds(pl.multiple_of(block * 256, 256), 256)


def pack_kernel(acts, cot, out, sems):
    core = lax.axis_index("core")
    copies = [
        pltpu.make_async_copy(
            acts.at[:, column(2 * k + 1 - core)], out.at[:, 256 * k : 256 * k + 256], sems.at[k]
        )
        for k in range(8)
    ] + [pltpu.make_async_copy(cot, out.at[:, 2048:], sems.at[8])]
    for copy in copies:
        copy.start()
    for copy in copies:
        copy.wait()


def fold_kernel(weight, globe, momentum, *rest):
    out = rest[-1]
    row = lax.axis_index(REP) * 8
    share = share_of(globe[0, 0], momentum[0, 0]) / SCALE
    out[...] = weight[0]
    start = pl.multiple_of(row // 16 * 16, 16)
    half = lax.broadcasted_iota(jnp.int32, (2, 8, 512), 0) == lax.rem(row // 8, 2)
    put = jnp.where(half, share[None], 0.0).reshape(16, 512)
    out[pl.ds(start, 16), :] = (weight[0, pl.ds(start, 16), :].astype(F32) + put).astype(BF)


def spread_kernel(scale, parts, *rest):
    out = rest[-1]
    total = parts[0].astype(F32)
    for k in range(1, parts.shape[0]):
        total += parts[k].astype(F32)
    total = (scale * total).astype(BF)
    for k in range(out.shape[0]):
        out[k] = total


def term(acts, cot, other, block, half):
    dims = (((0,), (0,)), ((), ()))
    return lax.dot_general(
        acts[:, column(block)], cot[...], dims, preferred_element_type=F32
    ) + lax.dot_general(other[:, column(half)], other[:, 2048:], dims, preferred_element_type=F32)


def sent_kernel(acts, cot, other, *rest):
    out = rest[-1]
    core, yhi = lax.axis_index("core"), 1 - lax.axis_index("yhi")
    for x in range(4):
        out[x] = term(acts, cot, other, 4 * x + 2 * yhi + core, 2 * x + yhi).astype(BF)


def kept_kernel(acts, cot, other, came, *outs):
    core, yhi, x = (lax.axis_index(n) for n in ("core", "yhi", "x"))
    for shift, out in enumerate(outs):
        to = lax.rem(x + shift, 4)
        total = term(acts, cot, other, 4 * to + 2 * yhi + core, 2 * to + yhi)
        out[...] = (total + came[to].astype(F32)).astype(BF)


def input_kernel(cot, other, *refs):
    pairs, (own, mate) = refs[:4], refs[-2:]
    tokens = cot.shape[0]
    left = jnp.concatenate([cot[...], other[:, 2048:]], 0)
    x, yhi = lax.axis_index("x"), lax.axis_index("yhi")
    for shift in range(4):
        for k in range(2):
            spot = column(2 * lax.rem(x + 4 - shift, 4) + (yhi if k == 0 else 1 - yhi))
            both = lax.dot_general(
                left, pairs[shift][k], (((1,), (1,)), ((), ())), preferred_element_type=F32
            ).astype(BF)
            own[:, spot] = both[:tokens]
            mate[:, spot] = both[tokens:]


def join_kernel(own, mate, *rest):
    out = rest[-1]
    core = lax.axis_index("core")
    for k in range(8):
        out[:, column(2 * k + core)] = own[:, 256 * k : 256 * k + 256]
        out[:, column(2 * k + 1 - core)] = mate[:, 256 * k : 256 * k + 256]


def finish_kernel(t0, t1, t2, t3, weight, adam_first, adam_second, rows, *outs):
    new_weight, new_first, new_second = outs
    grads = t0[...].astype(F32) + t1[...].astype(F32) + t2[...].astype(F32) + t3[...].astype(F32)
    wide = weight[0].astype(F32)
    first = beta_first * adam_first[0].astype(F32) + (1.0 - beta_first) * grads
    second = beta_second * adam_second[0].astype(F32) + (1.0 - beta_second) * grads * grads
    first_hat = first / (1.0 - beta_first**STEP)
    second_hat = second / (1.0 - beta_second**STEP)
    adamw = wide - inner_rate * (
        first_hat / (jnp.sqrt(second_hat) + epsilon_adam) + decay_rate * wide
    )
    new_weight[0] = (mix_factor * adamw + (1.0 - mix_factor) * rows[...].astype(F32)).astype(BF)
    new_first[0] = first.astype(BF)
    new_second[0] = second.astype(BF)


def finish(terms, weight, adam_first, adam_second, rows):
    size = 64
    state = pl.BlockSpec((1, size, 512), lambda j: (0, j, 0))
    return pl.pallas_call(
        finish_kernel,
        grid=(256 // size,),
        in_specs=[
            *[pl.BlockSpec((size, 512), lambda j: (j, 0))] * 4,
            *[state] * 3,
            pl.BlockSpec((size, 512), lambda j: (j, 0)),
        ],
        out_specs=[state] * 3,
        out_shape=[jax.ShapeDtypeStruct((1, 256, 512), BF)] * 3,
        compiler_params=pltpu.CompilerParams(vmem_limit_bytes=16 * 2**20),
        cost_estimate=pl.CostEstimate(flops=0, bytes_accessed=2**18, transcendentals=0),
        name="adam_and_mix",
    )(*terms, weight, adam_first, adam_second, rows)


def shards(acts, cot, inner_weight, adam_first, adam_second, global_weight, outer_momentum):
    weight = inner_weight[0]
    tokens = acts.shape[0]

    across = permute(weight, "yhi", 2, 1)

    packed = call(
        pack_kernel,
        (acts, cot),
        shaped(tokens, 2560),
        "pack", limit=60,
        loose=2,
        scratch=[pltpu.SemaphoreType.DMA((9,))],
        space=pltpu.HBM,
    )
    other = permute(packed, "core", 2, 1)

    blocks = call(
        fold_kernel,
        (inner_weight, global_weight, outer_momentum),
        shaped(256, 512),
        "fold_outer_state",
    )
    near = ("ylo", "zlo")
    parts = lax.all_to_all(blocks.reshape(8, 32, 512), near, 0, 0, tiled=True)
    send = call(
        sent_kernel, (acts, cot, other, blocks, across), shaped(4, 256, 512), "sent_terms", loose=2
    )
    came = permute(send, "yhi", 2, 1)

    keep = call(kept_kernel, (acts, cot, other, came), [shaped(256, 512)] * 4, "kept_terms")
    terms = [keep[0]] + [permute(keep[s], "x", 4, s) for s in (1, 3, 2)]

    pair = jnp.stack([weight, across])
    pairs = [pair] + [permute(pair, "x", 4, s) for s in (1, 3, 2)]
    pairs = [pairs[0], pairs[1], pairs[3], pairs[2]]

    parts = call(functools.partial(spread_kernel, 1.0), (parts,), shaped(4, 32, 512), "near_sum", weight=2000000000)
    parts = lax.all_to_all(parts, "zhi", 0, 0, tiled=True)
    mine, sent = call(
        input_kernel,
        (cot, other, *pairs),
        [shaped(tokens, 2048)] * 2,
        "input_grad_columns",
        loose=0,
    )
    rows = call(
        functools.partial(spread_kernel, SCALE),
        (parts, terms[1], terms[2], terms[3], sent),
        shaped(8, 32, 512),
        "far_sum",
        loose=4,
    )
    rows = lax.all_to_all(rows, near, 0, 0, tiled=True).reshape(256, 512)

    globe, momentum = global_weight[0, 0], outer_momentum[0, 0]
    own = lax.dynamic_slice_in_dim(rows, lax.axis_index(REP) * 8, 8, 0).astype(F32)
    outer_delta = globe - (own - share_of(globe, momentum)) / (32 * SCALE)
    momentum_new = momentum_coef * momentum + outer_delta
    global_new = globe - outer_rate * (outer_delta + momentum_coef * momentum_new)

    mate = permute(sent, "core", 2, 1)
    input_grad = call(
        join_kernel, (mine, mate), shaped(tokens, 4096), "input_grad", loose=0
    )

    new_weight, new_first, new_second = finish(
        terms, inner_weight, adam_first, adam_second, rows
    )
    return (
        input_grad,
        new_weight,
        new_first,
        new_second,
        global_new[None, None],
        momentum_new[None, None],
    )


def solution(mesh):
    return jax.shard_map(
        shards,
        mesh=Mesh(mesh.devices.reshape(SIZES), AXES),
        in_specs=(
            P(REP + FSDP, None),
            P(REP + FSDP, None),
            P(REP, FSDP, None),
            P(REP, FSDP, None),
            P(REP, FSDP, None),
            P(FSDP, REP, None, None),
            P(FSDP, REP, None, None),
        ),
        out_specs=(
            P(REP + FSDP, None),
            P(REP, FSDP, None),
            P(REP, FSDP, None),
            P(REP, FSDP, None),
            P(FSDP, REP, None, None),
            P(FSDP, REP, None, None),
        ),
        check_vma=False,
    )
```

```python
import functools

import jax
import jax.numpy as jnp
from jax import lax
from jax.experimental import pallas as pl
from jax.experimental.pallas import tpu as pltpu
from jax.sharding import Mesh, PartitionSpec as P

STEP = 10

momentum_coef = 0.9
outer_rate = 0.7
beta_first = 0.9
beta_second = 0.95
inner_rate = 0.25
decay_rate = 0.1
epsilon_adam = 1e-08
mix_factor = 0.5

AXES = ("ylo", "zhi", "zlo", "x", "yhi", "core")
SIZES = (2, 4, 4, 4, 2, 2)
REP = ("ylo", "zhi", "zlo")
FSDP = ("x", "yhi", "core")
BF = jnp.bfloat16
F32 = jnp.float32


def permute(array, axis, size, shift):
    return lax.ppermute(array, axis, [(i, (i + shift) % size) for i in range(size)])


SCALE = outer_rate * (1.0 + momentum_coef) / 32


def share_of(globe, momentum):
    return (1.0 - outer_rate * (1.0 + momentum_coef)) * globe - (
        outer_rate * momentum_coef * momentum_coef
    ) * momentum


def call(kernel, operands, out_shape, name, loose=0, scratch=(), space=pl.ANY, weight=0, limit=40):
    fixed = len(operands) - loose
    return pl.pallas_call(
        kernel,
        in_specs=[pl.BlockSpec(memory_space=pltpu.VMEM)] * fixed
        + [pl.BlockSpec(memory_space=space)] * loose,
        out_shape=out_shape,
        scratch_shapes=scratch,
        compiler_params=pltpu.CompilerParams(vmem_limit_bytes=limit * 2**20),
        cost_estimate=pl.CostEstimate(flops=weight, bytes_accessed=2**18, transcendentals=0),
        name=name,
    )(*operands)


def shaped(*shape):
    return jax.ShapeDtypeStruct(shape, BF)


def column(block):
    return pl.ds(pl.multiple_of(block * 256, 256), 256)


def pack_kernel(acts, cot, out, sems):
    core = lax.axis_index("core")
    copies = [
        pltpu.make_async_copy(
            acts.at[:, column(2 * k + 1 - core)], out.at[:, 256 * k : 256 * k + 256], sems.at[k]
        )
        for k in range(8)
    ] + [pltpu.make_async_copy(cot, out.at[:, 2048:], sems.at[8])]
    for copy in copies:
        copy.start()
    for copy in copies:
        copy.wait()


def fold_kernel(weight, globe, momentum, *rest):
    out = rest[-1]
    row = lax.axis_index(REP) * 8
    share = share_of(globe[0, 0], momentum[0, 0]) / SCALE
    out[...] = weight[0]
    start = pl.multiple_of(row // 16 * 16, 16)
    half = lax.broadcasted_iota(jnp.int32, (2, 8, 512), 0) == lax.rem(row // 8, 2)
    put = jnp.where(half, share[None], 0.0).reshape(16, 512)
    out[pl.ds(start, 16), :] = (weight[0, pl.ds(start, 16), :].astype(F32) + put).astype(BF)


def spread_kernel(scale, parts, *rest):
    out = rest[-1]
    total = parts[0].astype(F32)
    for k in range(1, parts.shape[0]):
        total += parts[k].astype(F32)
    total = (scale * total).astype(BF)
    for k in range(out.shape[0]):
        out[k] = total


def term(acts, cot, other, block, half):
    dims = (((0,), (0,)), ((), ()))
    return lax.dot_general(
        acts[:, column(block)], cot[...], dims, preferred_element_type=F32
    ) + lax.dot_general(other[:, column(half)], other[:, 2048:], dims, preferred_element_type=F32)


def sent_kernel(acts, cot, other, *rest):
    out = rest[-1]
    core, yhi = lax.axis_index("core"), 1 - lax.axis_index("yhi")
    for x in range(4):
        out[x] = term(acts, cot, other, 4 * x + 2 * yhi + core, 2 * x + yhi).astype(BF)


def kept_kernel(acts, cot, other, came, *outs):
    core, yhi, x = (lax.axis_index(n) for n in ("core", "yhi", "x"))
    for shift, out in enumerate(outs):
        to = lax.rem(x + shift, 4)
        total = term(acts, cot, other, 4 * to + 2 * yhi + core, 2 * to + yhi)
        out[...] = (total + came[to].astype(F32)).astype(BF)


def input_kernel(cot, other, *refs):
    pairs, (own, mate) = refs[:4], refs[-2:]
    tokens = cot.shape[0]
    left = jnp.concatenate([cot[...], other[:, 2048:]], 0)
    x, yhi = lax.axis_index("x"), lax.axis_index("yhi")
    for shift in range(4):
        for k in range(2):
            spot = column(2 * lax.rem(x + 4 - shift, 4) + (yhi if k == 0 else 1 - yhi))
            both = lax.dot_general(
                left, pairs[shift][k], (((1,), (1,)), ((), ())), preferred_element_type=F32
            ).astype(BF)
            own[:, spot] = both[:tokens]
            mate[:, spot] = both[tokens:]


def join_kernel(own, mate, *rest):
    out = rest[-1]
    core = lax.axis_index("core")
    for k in range(8):
        out[:, column(2 * k + core)] = own[:, 256 * k : 256 * k + 256]
        out[:, column(2 * k + 1 - core)] = mate[:, 256 * k : 256 * k + 256]


def adam_kernel(t0, t1, t2, t3, weight, adam_first, adam_second, half, new_first, new_second):
    grads = t0[...].astype(F32) + t1[...].astype(F32) + t2[...].astype(F32) + t3[...].astype(F32)
    wide = weight[0].astype(F32)
    first = beta_first * adam_first[0].astype(F32) + (1.0 - beta_first) * grads
    second = beta_second * adam_second[0].astype(F32) + (1.0 - beta_second) * grads * grads
    first_hat = first / (1.0 - beta_first**STEP)
    second_hat = second / (1.0 - beta_second**STEP)
    adamw = wide - inner_rate * (
        first_hat / (jnp.sqrt(second_hat) + epsilon_adam) + decay_rate * wide
    )
    half[...] = mix_factor * adamw
    new_first[0] = first.astype(BF)
    new_second[0] = second.astype(BF)


def mix_kernel(half, rows, globe, momentum, new_weight, new_global, new_momentum):
    new_weight[0] = (half[...] + (1.0 - mix_factor) * rows[...].astype(F32)).astype(BF)

    row = lax.axis_index(REP)
    two = rows[pl.ds(pl.multiple_of(row // 2 * 16, 16), 16), :].astype(F32).reshape(2, 8, 512)
    own = jnp.where(lax.rem(row, 2) == 0, two[0], two[1])
    outer_delta = globe[0, 0] - (own - share_of(globe[0, 0], momentum[0, 0])) / (32 * SCALE)
    momentum_new = momentum_coef * momentum[0, 0] + outer_delta
    new_global[0, 0] = globe[0, 0] - outer_rate * (outer_delta + momentum_coef * momentum_new)
    new_momentum[0, 0] = momentum_new


def shards(acts, cot, inner_weight, adam_first, adam_second, global_weight, outer_momentum):
    weight = inner_weight[0]
    tokens = acts.shape[0]

    across = permute(weight, "yhi", 2, 1)

    packed = call(
        pack_kernel,
        (acts, cot),
        shaped(tokens, 2560),
        "pack", limit=60,
        loose=2,
        scratch=[pltpu.SemaphoreType.DMA((9,))],
        space=pltpu.HBM,
    )
    other = permute(packed, "core", 2, 1)

    blocks = call(
        fold_kernel,
        (inner_weight, global_weight, outer_momentum),
        shaped(256, 512),
        "fold_outer_state",
    )
    near = ("ylo", "zlo")
    parts = lax.all_to_all(blocks.reshape(8, 32, 512), near, 0, 0, tiled=True)
    send = call(
        sent_kernel, (acts, cot, other, across), shaped(4, 256, 512), "sent_terms", weight=2000000000, loose=1
    )
    came = permute(send, "yhi", 2, 1)

    keep = call(kept_kernel, (acts, cot, other, came), [shaped(256, 512)] * 4, "kept_terms", weight=1000000000)
    terms = [keep[0]] + [permute(keep[s], "x", 4, s) for s in (1, 3, 2)]

    pair = jnp.stack([weight, across])
    pairs = [pair] + [permute(pair, "x", 4, s) for s in (1, 3, 2)]
    pairs = [pairs[0], pairs[1], pairs[3], pairs[2]]

    parts = call(functools.partial(spread_kernel, 1.0), (parts,), shaped(4, 32, 512), "near_sum", weight=1000000000)
    parts = lax.all_to_all(parts, "zhi", 0, 0, tiled=True)
    mine, sent = call(
        input_kernel,
        (cot, other, *pairs, keep[0]),
        [shaped(tokens, 2048)] * 2,
        "input_grad_columns",
        loose=1,
    )
    rows = call(
        functools.partial(spread_kernel, SCALE),
        (parts, sent),
        shaped(8, 32, 512),
        "far_sum",
        loose=1,
    )
    rows = lax.all_to_all(rows, near, 0, 0, tiled=True).reshape(256, 512)

    mate = permute(sent, "core", 2, 1)
    input_grad = call(
        join_kernel, (mine, mate), shaped(tokens, 4096), "input_grad", weight=500000000, loose=0
    )

    half, new_first, new_second = call(
        adam_kernel,
        (*terms, inner_weight, adam_first, adam_second),
        [jax.ShapeDtypeStruct((256, 512), F32)] + [shaped(1, 256, 512)] * 2,
        "adam", weight=8000000000,
    )
    outer = jax.ShapeDtypeStruct((1, 1, 8, 512), F32)
    new_weight, new_global, new_momentum = call(
        mix_kernel,
        (half, rows, global_weight, outer_momentum),
        [shaped(1, 256, 512), outer, outer],
        "mix", weight=500000000,
    )
    return input_grad, new_weight, new_first, new_second, new_global, new_momentum


def solution(mesh):
    return jax.shard_map(
        shards,
        mesh=Mesh(mesh.devices.reshape(SIZES), AXES),
        in_specs=(
            P(REP + FSDP, None),
            P(REP + FSDP, None),
            P(REP, FSDP, None),
            P(REP, FSDP, None),
            P(REP, FSDP, None),
            P(FSDP, REP, None, None),
            P(FSDP, REP, None, None),
        ),
        out_specs=(
            P(REP + FSDP, None),
            P(REP, FSDP, None),
            P(REP, FSDP, None),
            P(REP, FSDP, None),
            P(FSDP, REP, None, None),
            P(FSDP, REP, None, None),
        ),
        check_vma=False,
    )
```

```python
import functools

import jax
import jax.numpy as jnp
from jax import lax
from jax.experimental import pallas as pl
from jax.experimental.pallas import tpu as pltpu
from jax.sharding import Mesh, PartitionSpec as P

STEP = 10

momentum_coef = 0.9
outer_rate = 0.7
beta_first = 0.9
beta_second = 0.95
inner_rate = 0.25
decay_rate = 0.1
epsilon_adam = 1e-08
mix_factor = 0.5

AXES = ("ylo", "zhi", "zlo", "x", "yhi", "core")
SIZES = (2, 4, 4, 4, 2, 2)
REP = ("ylo", "zhi", "zlo")
FSDP = ("x", "yhi", "core")
BF = jnp.bfloat16
F32 = jnp.float32


def permute(array, axis, size, shift):
    return lax.ppermute(array, axis, [(i, (i + shift) % size) for i in range(size)])


SCALE = outer_rate * (1.0 + momentum_coef) / 32


def share_of(globe, momentum):
    return (1.0 - outer_rate * (1.0 + momentum_coef)) * globe - (
        outer_rate * momentum_coef * momentum_coef
    ) * momentum


def call(kernel, operands, out_shape, name, loose=0, scratch=(), space=pl.ANY, weight=0, limit=40):
    fixed = len(operands) - loose
    return pl.pallas_call(
        kernel,
        in_specs=[pl.BlockSpec(memory_space=pltpu.VMEM)] * fixed
        + [pl.BlockSpec(memory_space=space)] * loose,
        out_shape=out_shape,
        scratch_shapes=scratch,
        compiler_params=pltpu.CompilerParams(vmem_limit_bytes=limit * 2**20),
        cost_estimate=pl.CostEstimate(flops=weight, bytes_accessed=2**18, transcendentals=0),
        name=name,
    )(*operands)


def shaped(*shape):
    return jax.ShapeDtypeStruct(shape, BF)


def column(block):
    return pl.ds(pl.multiple_of(block * 256, 256), 256)


def pack_kernel(acts, cot, out, sems):
    core = lax.axis_index("core")
    copies = [
        pltpu.make_async_copy(
            acts.at[:, column(2 * k + 1 - core)], out.at[:, 256 * k : 256 * k + 256], sems.at[k]
        )
        for k in range(8)
    ] + [pltpu.make_async_copy(cot, out.at[:, 2048:], sems.at[8])]
    for copy in copies:
        copy.start()
    for copy in copies:
        copy.wait()


def fold_kernel(weight, globe, momentum, *rest):
    out = rest[-1]
    row = lax.axis_index(REP) * 8
    share = share_of(globe[0, 0], momentum[0, 0]) / SCALE
    out[...] = weight[0]
    start = pl.multiple_of(row // 16 * 16, 16)
    half = lax.broadcasted_iota(jnp.int32, (2, 8, 512), 0) == lax.rem(row // 8, 2)
    put = jnp.where(half, share[None], 0.0).reshape(16, 512)
    out[pl.ds(start, 16), :] = (weight[0, pl.ds(start, 16), :].astype(F32) + put).astype(BF)


def spread_kernel(scale, parts, *rest):
    out = rest[-1]
    total = parts[0].astype(F32)
    for k in range(1, parts.shape[0]):
        total += parts[k].astype(F32)
    total = (scale * total).astype(BF)
    for k in range(out.shape[0]):
        out[k] = total


def term(acts, cot, other, block, half):
    dims = (((0,), (0,)), ((), ()))
    return lax.dot_general(
        acts[:, column(block)], cot[...], dims, preferred_element_type=F32
    ) + lax.dot_general(other[:, column(half)], other[:, 2048:], dims, preferred_element_type=F32)


def sent_kernel(acts, cot, other, *rest):
    out = rest[-1]
    core, yhi = lax.axis_index("core"), 1 - lax.axis_index("yhi")
    for x in range(4):
        out[x] = term(acts, cot, other, 4 * x + 2 * yhi + core, 2 * x + yhi).astype(BF)


def kept_kernel(acts, cot, other, came, *outs):
    core, yhi, x = (lax.axis_index(n) for n in ("core", "yhi", "x"))
    for shift, out in enumerate(outs):
        to = lax.rem(x + shift, 4)
        total = term(acts, cot, other, 4 * to + 2 * yhi + core, 2 * to + yhi)
        out[...] = (total + came[to].astype(F32)).astype(BF)


def input_kernel(cot, other, *refs):
    pairs, (own, mate) = refs[:4], refs[-2:]
    tokens = cot.shape[0]
    left = jnp.concatenate([cot[...], other[:, 2048:]], 0)
    x, yhi = lax.axis_index("x"), lax.axis_index("yhi")
    for shift in range(4):
        for k in range(2):
            spot = column(2 * lax.rem(x + 4 - shift, 4) + (yhi if k == 0 else 1 - yhi))
            both = lax.dot_general(
                left, pairs[shift][k], (((1,), (1,)), ((), ())), preferred_element_type=F32
            ).astype(BF)
            own[:, spot] = both[:tokens]
            mate[:, spot] = both[tokens:]


def join_kernel(own, mate, *rest):
    out = rest[-1]
    core = lax.axis_index("core")
    for k in range(8):
        out[:, column(2 * k + core)] = own[:, 256 * k : 256 * k + 256]
        out[:, column(2 * k + 1 - core)] = mate[:, 256 * k : 256 * k + 256]


def adam_kernel(t0, t1, t2, t3, weight, adam_first, adam_second, half, new_first, new_second):
    grads = t0[...].astype(F32) + t1[...].astype(F32) + t2[...].astype(F32) + t3[...].astype(F32)
    wide = weight[0].astype(F32)
    first = beta_first * adam_first[0].astype(F32) + (1.0 - beta_first) * grads
    second = beta_second * adam_second[0].astype(F32) + (1.0 - beta_second) * grads * grads
    first_hat = first / (1.0 - beta_first**STEP)
    second_hat = second / (1.0 - beta_second**STEP)
    adamw = wide - inner_rate * (
        first_hat / (jnp.sqrt(second_hat) + epsilon_adam) + decay_rate * wide
    )
    half[...] = mix_factor * adamw
    new_first[0] = first.astype(BF)
    new_second[0] = second.astype(BF)


def mix_kernel(half, rows, globe, momentum, new_weight, new_global, new_momentum):
    new_weight[0] = (half[...] + (1.0 - mix_factor) * rows[...].astype(F32)).astype(BF)

    row = lax.axis_index(REP)
    two = rows[pl.ds(pl.multiple_of(row // 2 * 16, 16), 16), :].astype(F32).reshape(2, 8, 512)
    own = jnp.where(lax.rem(row, 2) == 0, two[0], two[1])
    outer_delta = globe[0, 0] - (own - share_of(globe[0, 0], momentum[0, 0])) / (32 * SCALE)
    momentum_new = momentum_coef * momentum[0, 0] + outer_delta
    new_global[0, 0] = globe[0, 0] - outer_rate * (outer_delta + momentum_coef * momentum_new)
    new_momentum[0, 0] = momentum_new


def shards(acts, cot, inner_weight, adam_first, adam_second, global_weight, outer_momentum):
    weight = inner_weight[0]
    tokens = acts.shape[0]

    across = permute(weight, "yhi", 2, 1)

    packed = call(
        pack_kernel,
        (acts, cot),
        shaped(tokens, 2560),
        "pack", weight=500000000, limit=60,
        loose=2,
        scratch=[pltpu.SemaphoreType.DMA((9,))],
        space=pltpu.HBM,
    )
    other = permute(packed, "core", 2, 1)

    blocks = call(
        fold_kernel,
        (inner_weight, global_weight, outer_momentum),
        shaped(256, 512),
        "fold_outer_state",
    )
    near = ("ylo", "zlo")
    parts = lax.all_to_all(blocks.reshape(8, 32, 512), near, 0, 0, tiled=True)
    send = call(
        sent_kernel, (acts, cot, other, blocks, across), shaped(4, 256, 512), "sent_terms", weight=500000000, loose=2
    )
    came = permute(send, "yhi", 2, 1)

    keep = call(kept_kernel, (acts, cot, other, came), [shaped(256, 512)] * 4, "kept_terms", weight=1000000000)
    terms = [keep[0]] + [permute(keep[s], "x", 4, s) for s in (1, 3, 2)]

    pair = jnp.stack([weight, across])
    pairs = [pair] + [permute(pair, "x", 4, s) for s in (1, 3, 2)]
    pairs = [pairs[0], pairs[1], pairs[3], pairs[2]]

    parts = call(functools.partial(spread_kernel, 1.0), (parts,), shaped(4, 32, 512), "near_sum")
    parts = lax.all_to_all(parts, "zhi", 0, 0, tiled=True)
    mine, sent = call(
        input_kernel,
        (cot, other, *pairs, parts, keep[1]),
        [shaped(tokens, 2048)] * 2,
        "input_grad_columns",
        loose=2,
    )
    rows = call(
        functools.partial(spread_kernel, SCALE),
        (parts, keep[1]),
        shaped(8, 32, 512),
        "far_sum",
        loose=1,
    )
    rows = lax.all_to_all(rows, near, 0, 0, tiled=True).reshape(256, 512)

    mate = permute(sent, "core", 2, 1)
    input_grad = call(
        join_kernel, (mine, mate), shaped(tokens, 4096), "input_grad", loose=0
    )

    half, new_first, new_second = call(
        adam_kernel,
        (*terms, inner_weight, adam_first, adam_second),
        [jax.ShapeDtypeStruct((256, 512), F32)] + [shaped(1, 256, 512)] * 2,
        "adam", weight=8000000000,
    )
    outer = jax.ShapeDtypeStruct((1, 1, 8, 512), F32)
    new_weight, new_global, new_momentum = call(
        mix_kernel,
        (half, rows, global_weight, outer_momentum),
        [shaped(1, 256, 512), outer, outer],
        "mix", weight=4000000000,
    )
    return input_grad, new_weight, new_first, new_second, new_global, new_momentum


def solution(mesh):
    return jax.shard_map(
        shards,
        mesh=Mesh(mesh.devices.reshape(SIZES), AXES),
        in_specs=(
            P(REP + FSDP, None),
            P(REP + FSDP, None),
            P(REP, FSDP, None),
            P(REP, FSDP, None),
            P(REP, FSDP, None),
            P(FSDP, REP, None, None),
            P(FSDP, REP, None, None),
        ),
        out_specs=(
            P(REP + FSDP, None),
            P(REP, FSDP, None),
            P(REP, FSDP, None),
            P(REP, FSDP, None),
            P(FSDP, REP, None, None),
            P(FSDP, REP, None, None),
        ),
        check_vma=False,
    )
```

```python
import functools

import jax
import jax.numpy as jnp
from jax import lax
from jax.experimental import pallas as pl
from jax.experimental.pallas import tpu as pltpu
from jax.sharding import Mesh, PartitionSpec as P

STEP = 10

momentum_coef = 0.9
outer_rate = 0.7
beta_first = 0.9
beta_second = 0.95
inner_rate = 0.25
decay_rate = 0.1
epsilon_adam = 1e-08
mix_factor = 0.5

AXES = ("ylo", "zhi", "zlo", "x", "yhi", "core")
SIZES = (2, 4, 4, 4, 2, 2)
REP = ("ylo", "zhi", "zlo")
FSDP = ("x", "yhi", "core")
BF = jnp.bfloat16
F32 = jnp.float32


def permute(array, axis, size, shift):
    return lax.ppermute(array, axis, [(i, (i + shift) % size) for i in range(size)])


SCALE = outer_rate * (1.0 + momentum_coef) / 32


def share_of(globe, momentum):
    return (1.0 - outer_rate * (1.0 + momentum_coef)) * globe - (
        outer_rate * momentum_coef * momentum_coef
    ) * momentum


def call(kernel, operands, out_shape, name, loose=0, scratch=(), space=pl.ANY, weight=0, limit=40):
    fixed = len(operands) - loose
    return pl.pallas_call(
        kernel,
        in_specs=[pl.BlockSpec(memory_space=pltpu.VMEM)] * fixed
        + [pl.BlockSpec(memory_space=space)] * loose,
        out_shape=out_shape,
        scratch_shapes=scratch,
        compiler_params=pltpu.CompilerParams(vmem_limit_bytes=limit * 2**20),
        cost_estimate=pl.CostEstimate(flops=weight, bytes_accessed=2**18, transcendentals=0),
        name=name,
    )(*operands)


def shaped(*shape):
    return jax.ShapeDtypeStruct(shape, BF)


def column(block):
    return pl.ds(pl.multiple_of(block * 256, 256), 256)


def pack_kernel(acts, cot, out, sems):
    core = lax.axis_index("core")
    copies = [
        pltpu.make_async_copy(
            acts.at[:, column(2 * k + 1 - core)], out.at[:, 256 * k : 256 * k + 256], sems.at[k]
        )
        for k in range(8)
    ] + [pltpu.make_async_copy(cot, out.at[:, 2048:], sems.at[8])]
    for copy in copies:
        copy.start()
    for copy in copies:
        copy.wait()


def fold_kernel(weight, globe, momentum, *rest):
    out = rest[-1]
    row = lax.axis_index(REP) * 8
    share = share_of(globe[0, 0], momentum[0, 0]) / SCALE
    out[...] = weight[0]
    start = pl.multiple_of(row // 16 * 16, 16)
    half = lax.broadcasted_iota(jnp.int32, (2, 8, 512), 0) == lax.rem(row // 8, 2)
    put = jnp.where(half, share[None], 0.0).reshape(16, 512)
    out[pl.ds(start, 16), :] = (weight[0, pl.ds(start, 16), :].astype(F32) + put).astype(BF)


def spread_kernel(scale, parts, *rest):
    out = rest[-1]
    total = parts[0].astype(F32)
    for k in range(1, parts.shape[0]):
        total += parts[k].astype(F32)
    total = (scale * total).astype(BF)
    for k in range(out.shape[0]):
        out[k] = total


def term(acts, cot, other, block, half):
    dims = (((0,), (0,)), ((), ()))
    return lax.dot_general(
        acts[:, column(block)], cot[...], dims, preferred_element_type=F32
    ) + lax.dot_general(other[:, column(half)], other[:, 2048:], dims, preferred_element_type=F32)


def sent_kernel(acts, cot, other, *rest):
    out = rest[-1]
    core, yhi = lax.axis_index("core"), 1 - lax.axis_index("yhi")
    for x in range(4):
        out[x] = term(acts, cot, other, 4 * x + 2 * yhi + core, 2 * x + yhi).astype(BF)


def kept_kernel(acts, cot, other, came, *outs):
    core, yhi, x = (lax.axis_index(n) for n in ("core", "yhi", "x"))
    for shift, out in enumerate(outs):
        to = lax.rem(x + shift, 4)
        total = term(acts, cot, other, 4 * to + 2 * yhi + core, 2 * to + yhi)
        out[...] = (total + came[to].astype(F32)).astype(BF)


def input_kernel(cot, other, *refs):
    pairs, (own, mate) = refs[:4], refs[-2:]
    tokens = cot.shape[0]
    left = jnp.concatenate([cot[...], other[:, 2048:]], 0)
    x, yhi = lax.axis_index("x"), lax.axis_index("yhi")
    for shift in range(4):
        for k in range(2):
            spot = column(2 * lax.rem(x + 4 - shift, 4) + (yhi if k == 0 else 1 - yhi))
            both = lax.dot_general(
                left, pairs[shift][k], (((1,), (1,)), ((), ())), preferred_element_type=F32
            ).astype(BF)
            own[:, spot] = both[:tokens]
            mate[:, spot] = both[tokens:]


def pair_kernel(own, across, _, out):
    out[0], out[1] = own[...], across[...]


def join_kernel(own, mate, *rest):
    out = rest[-1]
    core = lax.axis_index("core")
    for k in range(8):
        out[:, column(2 * k + core)] = own[:, 256 * k : 256 * k + 256]
        out[:, column(2 * k + 1 - core)] = mate[:, 256 * k : 256 * k + 256]


def adam_kernel(t0, t1, t2, t3, weight, adam_first, adam_second, half, new_first, new_second):
    grads = t0[...].astype(F32) + t1[...].astype(F32) + t2[...].astype(F32) + t3[...].astype(F32)
    wide = weight[0].astype(F32)
    first = beta_first * adam_first[0].astype(F32) + (1.0 - beta_first) * grads
    second = beta_second * adam_second[0].astype(F32) + (1.0 - beta_second) * grads * grads
    first_hat = first / (1.0 - beta_first**STEP)
    second_hat = second / (1.0 - beta_second**STEP)
    adamw = wide - inner_rate * (
        first_hat / (jnp.sqrt(second_hat) + epsilon_adam) + decay_rate * wide
    )
    half[...] = mix_factor * adamw
    new_first[0] = first.astype(BF)
    new_second[0] = second.astype(BF)


def mix_kernel(half, rows, globe, momentum, new_weight, new_global, new_momentum):
    new_weight[0] = (half[...] + (1.0 - mix_factor) * rows[...].astype(F32)).astype(BF)

    row = lax.axis_index(REP)
    two = rows[pl.ds(pl.multiple_of(row // 2 * 16, 16), 16), :].astype(F32).reshape(2, 8, 512)
    own = jnp.where(lax.rem(row, 2) == 0, two[0], two[1])
    outer_delta = globe[0, 0] - (own - share_of(globe[0, 0], momentum[0, 0])) / (32 * SCALE)
    momentum_new = momentum_coef * momentum[0, 0] + outer_delta
    new_global[0, 0] = globe[0, 0] - outer_rate * (outer_delta + momentum_coef * momentum_new)
    new_momentum[0, 0] = momentum_new


def shards(acts, cot, inner_weight, adam_first, adam_second, global_weight, outer_momentum):
    weight = inner_weight[0]
    tokens = acts.shape[0]

    across = permute(weight, "yhi", 2, 1)

    packed = call(
        pack_kernel,
        (acts, cot),
        shaped(tokens, 2560),
        "pack", weight=500000000, limit=60,
        loose=2,
        scratch=[pltpu.SemaphoreType.DMA((9,))],
        space=pltpu.HBM,
    )
    other = permute(packed, "core", 2, 1)

    blocks = call(
        fold_kernel,
        (inner_weight, global_weight, outer_momentum),
        shaped(256, 512),
        "fold_outer_state",
    )
    near = ("ylo", "zlo")
    parts = lax.all_to_all(blocks.reshape(8, 32, 512), near, 0, 0, tiled=True)
    send = call(
        sent_kernel, (acts, cot, other, blocks, across), shaped(4, 256, 512), "sent_terms", weight=500000000, loose=2
    )
    came = permute(send, "yhi", 2, 1)

    keep = call(kept_kernel, (acts, cot, other, came), [shaped(256, 512)] * 4, "kept_terms", weight=1000000000)
    terms = [keep[0]] + [permute(keep[s], "x", 4, s) for s in (1, 3, 2)]

    summed = call(functools.partial(spread_kernel, 1.0), (parts,), shaped(4, 32, 512), "near_sum")
    pair = call(pair_kernel, (weight, across, summed), shaped(2, 256, 512), "pair", loose=1)
    pairs = [pair] + [permute(pair, "x", 4, s) for s in (1, 3, 2)]
    pairs = [pairs[0], pairs[1], pairs[3], pairs[2]]

    parts = lax.all_to_all(summed, "zhi", 0, 0, tiled=True)
    mine, sent = call(
        input_kernel,
        (cot, other, *pairs, parts, keep[1]),
        [shaped(tokens, 2048)] * 2,
        "input_grad_columns",
        loose=2,
    )
    rows = call(
        functools.partial(spread_kernel, SCALE),
        (parts, keep[1]),
        shaped(8, 32, 512),
        "far_sum",
        loose=1,
    )
    rows = lax.all_to_all(rows, near, 0, 0, tiled=True).reshape(256, 512)

    mate = permute(sent, "core", 2, 1)
    input_grad = call(
        join_kernel, (mine, mate), shaped(tokens, 4096), "input_grad", loose=0
    )

    half, new_first, new_second = call(
        adam_kernel,
        (*terms, inner_weight, adam_first, adam_second),
        [jax.ShapeDtypeStruct((256, 512), F32)] + [shaped(1, 256, 512)] * 2,
        "adam", weight=8000000000,
    )
    outer = jax.ShapeDtypeStruct((1, 1, 8, 512), F32)
    new_weight, new_global, new_momentum = call(
        mix_kernel,
        (half, rows, global_weight, outer_momentum),
        [shaped(1, 256, 512), outer, outer],
        "mix", weight=4000000000,
    )
    return input_grad, new_weight, new_first, new_second, new_global, new_momentum


def solution(mesh):
    return jax.shard_map(
        shards,
        mesh=Mesh(mesh.devices.reshape(SIZES), AXES),
        in_specs=(
            P(REP + FSDP, None),
            P(REP + FSDP, None),
            P(REP, FSDP, None),
            P(REP, FSDP, None),
            P(REP, FSDP, None),
            P(FSDP, REP, None, None),
            P(FSDP, REP, None, None),
        ),
        out_specs=(
            P(REP + FSDP, None),
            P(REP, FSDP, None),
            P(REP, FSDP, None),
            P(REP, FSDP, None),
            P(FSDP, REP, None, None),
            P(FSDP, REP, None, None),
        ),
        check_vma=False,
    )
```

```python
import functools

import jax
import jax.numpy as jnp
from jax import lax
from jax.experimental import pallas as pl
from jax.experimental.pallas import tpu as pltpu
from jax.sharding import Mesh, PartitionSpec as P

STEP = 10

momentum_coef = 0.9
outer_rate = 0.7
beta_first = 0.9
beta_second = 0.95
inner_rate = 0.25
decay_rate = 0.1
epsilon_adam = 1e-08
mix_factor = 0.5

AXES = ("ylo", "zhi", "zlo", "x", "yhi", "core")
SIZES = (2, 4, 4, 4, 2, 2)
REP = ("ylo", "zhi", "zlo")
FSDP = ("x", "yhi", "core")
BF = jnp.bfloat16
F32 = jnp.float32


def permute(array, axis, size, shift):
    return lax.ppermute(array, axis, [(i, (i + shift) % size) for i in range(size)])


SCALE = outer_rate * (1.0 + momentum_coef) / 32


def share_of(globe, momentum):
    return (1.0 - outer_rate * (1.0 + momentum_coef)) * globe - (
        outer_rate * momentum_coef * momentum_coef
    ) * momentum


def call(kernel, operands, out_shape, name, loose=0, scratch=(), space=pl.ANY, weight=0, limit=40):
    fixed = len(operands) - loose
    return pl.pallas_call(
        kernel,
        in_specs=[pl.BlockSpec(memory_space=pltpu.VMEM)] * fixed
        + [pl.BlockSpec(memory_space=space)] * loose,
        out_shape=out_shape,
        scratch_shapes=scratch,
        compiler_params=pltpu.CompilerParams(vmem_limit_bytes=limit * 2**20),
        cost_estimate=pl.CostEstimate(flops=weight, bytes_accessed=2**18, transcendentals=0),
        name=name,
    )(*operands)


def shaped(*shape):
    return jax.ShapeDtypeStruct(shape, BF)


def column(block):
    return pl.ds(pl.multiple_of(block * 256, 256), 256)


def pack_kernel(acts, cot, out, sems):
    core = lax.axis_index("core")
    copies = [
        pltpu.make_async_copy(
            acts.at[:, column(2 * k + 1 - core)], out.at[:, 256 * k : 256 * k + 256], sems.at[k]
        )
        for k in range(8)
    ] + [pltpu.make_async_copy(cot, out.at[:, 2048:], sems.at[8])]
    for copy in copies:
        copy.start()
    for copy in copies:
        copy.wait()


def fold_kernel(weight, globe, momentum, *rest):
    out = rest[-1]
    row = lax.axis_index(REP) * 8
    share = share_of(globe[0, 0], momentum[0, 0]) / SCALE
    out[...] = weight[0]
    start = pl.multiple_of(row // 16 * 16, 16)
    half = lax.broadcasted_iota(jnp.int32, (2, 8, 512), 0) == lax.rem(row // 8, 2)
    put = jnp.where(half, share[None], 0.0).reshape(16, 512)
    out[pl.ds(start, 16), :] = (weight[0, pl.ds(start, 16), :].astype(F32) + put).astype(BF)


def spread_kernel(scale, parts, *rest):
    out = rest[-1]
    total = parts[0].astype(F32)
    for k in range(1, parts.shape[0]):
        total += parts[k].astype(F32)
    total = (scale * total).astype(BF)
    for k in range(out.shape[0]):
        out[k] = total


def term(acts, cot, other, block, half):
    dims = (((0,), (0,)), ((), ()))
    return lax.dot_general(
        acts[:, column(block)], cot[...], dims, preferred_element_type=F32
    ) + lax.dot_general(other[:, column(half)], other[:, 2048:], dims, preferred_element_type=F32)


def sent_kernel(acts, cot, other, *rest):
    out = rest[-1]
    core, yhi = lax.axis_index("core"), 1 - lax.axis_index("yhi")
    for x in range(4):
        out[x] = term(acts, cot, other, 4 * x + 2 * yhi + core, 2 * x + yhi).astype(BF)


def kept_kernel(acts, cot, other, came, *outs):
    core, yhi, x = (lax.axis_index(n) for n in ("core", "yhi", "x"))
    for shift, out in enumerate(outs):
        to = lax.rem(x + shift, 4)
        total = term(acts, cot, other, 4 * to + 2 * yhi + core, 2 * to + yhi)
        out[...] = (total + came[to].astype(F32)).astype(BF)


def input_kernel(cot, other, *refs):
    pairs, (own, mate) = refs[:4], refs[-2:]
    tokens = cot.shape[0]
    left = jnp.concatenate([cot[...], other[:, 2048:]], 0)
    x, yhi = lax.axis_index("x"), lax.axis_index("yhi")
    for shift in range(4):
        for k in range(2):
            spot = column(2 * lax.rem(x + 4 - shift, 4) + (yhi if k == 0 else 1 - yhi))
            both = lax.dot_general(
                left, pairs[shift][k], (((1,), (1,)), ((), ())), preferred_element_type=F32
            ).astype(BF)
            own[:, spot] = both[:tokens]
            mate[:, spot] = both[tokens:]


def pair_kernel(own, across, _, out):
    out[0], out[1] = own[...], across[...]


def join_kernel(own, mate, *rest):
    out = rest[-1]
    core = lax.axis_index("core")
    for k in range(8):
        out[:, column(2 * k + core)] = own[:, 256 * k : 256 * k + 256]
        out[:, column(2 * k + 1 - core)] = mate[:, 256 * k : 256 * k + 256]


def adam_kernel(t0, t1, t2, t3, weight, adam_first, adam_second, half, new_first, new_second):
    grads = t0[...].astype(F32) + t1[...].astype(F32) + t2[...].astype(F32) + t3[...].astype(F32)
    wide = weight[0].astype(F32)
    first = beta_first * adam_first[0].astype(F32) + (1.0 - beta_first) * grads
    second = beta_second * adam_second[0].astype(F32) + (1.0 - beta_second) * grads * grads
    first_hat = first / (1.0 - beta_first**STEP)
    second_hat = second / (1.0 - beta_second**STEP)
    adamw = wide - inner_rate * (
        first_hat / (jnp.sqrt(second_hat) + epsilon_adam) + decay_rate * wide
    )
    half[...] = mix_factor * adamw
    new_first[0] = first.astype(BF)
    new_second[0] = second.astype(BF)


def mix_kernel(half, rows, globe, momentum, new_weight, new_global, new_momentum):
    new_weight[0] = (half[...] + (1.0 - mix_factor) * rows[...].astype(F32)).astype(BF)

    row = lax.axis_index(REP)
    two = rows[pl.ds(pl.multiple_of(row // 2 * 16, 16), 16), :].astype(F32).reshape(2, 8, 512)
    own = jnp.where(lax.rem(row, 2) == 0, two[0], two[1])
    outer_delta = globe[0, 0] - (own - share_of(globe[0, 0], momentum[0, 0])) / (32 * SCALE)
    momentum_new = momentum_coef * momentum[0, 0] + outer_delta
    new_global[0, 0] = globe[0, 0] - outer_rate * (outer_delta + momentum_coef * momentum_new)
    new_momentum[0, 0] = momentum_new


def shards(acts, cot, inner_weight, adam_first, adam_second, global_weight, outer_momentum):
    weight = inner_weight[0]
    tokens = acts.shape[0]

    across = permute(weight, "yhi", 2, 1)

    packed = call(
        pack_kernel,
        (acts, cot),
        shaped(tokens, 2560),
        "pack", weight=500000000, limit=60,
        loose=2,
        scratch=[pltpu.SemaphoreType.DMA((9,))],
        space=pltpu.HBM,
    )
    other = permute(packed, "core", 2, 1)

    blocks = call(
        fold_kernel,
        (inner_weight, global_weight, outer_momentum),
        shaped(256, 512),
        "fold_outer_state",
    )
    near = ("ylo", "zlo")
    parts = lax.all_to_all(blocks.reshape(8, 32, 512), near, 0, 0, tiled=True)
    send = call(
        sent_kernel, (acts, cot, other, blocks, across), shaped(4, 256, 512), "sent_terms", weight=500000000, loose=2
    )
    came = permute(send, "yhi", 2, 1)

    keep = call(kept_kernel, (acts, cot, other, came), [shaped(256, 512)] * 4, "kept_terms", weight=1000000000)
    terms = [keep[0]] + [permute(keep[s], "x", 4, s) for s in (2, 1, 3)]

    summed = call(functools.partial(spread_kernel, 1.0), (parts,), shaped(4, 32, 512), "near_sum")
    pair = call(pair_kernel, (weight, across, summed), shaped(2, 256, 512), "pair", loose=1)
    pairs = [pair] + [permute(pair, "x", 4, s) for s in (1, 3, 2)]
    pairs = [pairs[0], pairs[1], pairs[3], pairs[2]]

    parts = lax.all_to_all(summed, "zhi", 0, 0, tiled=True)
    mine, sent = call(
        input_kernel,
        (cot, other, *pairs, parts, keep[1]),
        [shaped(tokens, 2048)] * 2,
        "input_grad_columns",
        loose=2,
    )
    rows = call(
        functools.partial(spread_kernel, SCALE),
        (parts, keep[1]),
        shaped(8, 32, 512),
        "far_sum",
        loose=1,
    )
    rows = lax.all_to_all(rows, near, 0, 0, tiled=True).reshape(256, 512)

    mate = permute(sent, "core", 2, 1)
    input_grad = call(
        join_kernel, (mine, mate), shaped(tokens, 4096), "input_grad", loose=0
    )

    half, new_first, new_second = call(
        adam_kernel,
        (*terms, inner_weight, adam_first, adam_second),
        [jax.ShapeDtypeStruct((256, 512), F32)] + [shaped(1, 256, 512)] * 2,
        "adam", weight=8000000000,
    )
    outer = jax.ShapeDtypeStruct((1, 1, 8, 512), F32)
    new_weight, new_global, new_momentum = call(
        mix_kernel,
        (half, rows, global_weight, outer_momentum),
        [shaped(1, 256, 512), outer, outer],
        "mix", weight=4000000000,
    )
    return input_grad, new_weight, new_first, new_second, new_global, new_momentum


def solution(mesh):
    return jax.shard_map(
        shards,
        mesh=Mesh(mesh.devices.reshape(SIZES), AXES),
        in_specs=(
            P(REP + FSDP, None),
            P(REP + FSDP, None),
            P(REP, FSDP, None),
            P(REP, FSDP, None),
            P(REP, FSDP, None),
            P(FSDP, REP, None, None),
            P(FSDP, REP, None, None),
        ),
        out_specs=(
            P(REP + FSDP, None),
            P(REP, FSDP, None),
            P(REP, FSDP, None),
            P(REP, FSDP, None),
            P(FSDP, REP, None, None),
            P(FSDP, REP, None, None),
        ),
        check_vma=False,
    )
```
